512 devices in a mesh: expert: 64 (over y, x, core), dp: 8 (over z).
Axes of the slice: x: 4, y: 8, z: 8, core: 2. Of those that a mesh axis runs over, the one named last changes fastest.
Arguments:
- layer_input: bfloat16 [65536, 2048], P(('expert', 'dp')), may hold values from -6 to 6
- log_grad: bfloat16 [65536, 2048], P(('expert', 'dp')), may hold values from -6 to 6
- router_logits: float32 [65536, 64], P(('expert', 'dp')), may hold values from -6 to 250
- expert_ids: int32 [65536, 1], P(('expert', 'dp')), may hold values from 0 to 63, as said below
- router_weight: bfloat16 [64, 2048], replicated, may hold values from -0.125 to 0.125
- gate_weight: bfloat16 [64, 2048, 1408], P('expert', None, 'dp'), may hold values from -0.125 to 0.125
- up_weight: bfloat16 [64, 2048, 1408], P('expert', None, 'dp'), may hold values from -0.125 to 0.125
- down_weight: bfloat16 [64, 1408, 2048], P('expert', 'dp'), may hold values from -0.15625 to 0.15625
- saved_pre: bfloat16 [64, 64, 8, 3, 2, 1408], P('expert', None, None, None, None, 'dp'), may hold values from -6 to 6
- request_ids: int32 [512], P(('expert', 'dp')), may hold values from 0 to 127, as said below
- risk_points: int32 [512], P(('expert', 'dp')), may hold values from 0 to 8000
- cand_scores: float32 [512], P(('expert', 'dp')), may hold values from -402 to 250
Outputs:
- input_grad: bfloat16 [65536, 2048], P(('expert', 'dp'))
- router_grad: float32 [64, 2048], P(None, ('expert', 'dp'))
The draws below stay inside these ranges and needn't reach their ends.
Inputs may be any that keep to these rules, and one draw needn't show every extreme that they name: `expert_ids`: in the rows of one candidate no expert appears more than 3 times, and one expert appears exactly 3 times in every candidate's rows. `request_ids`: every request id appears exactly 4 times.
All inputs are finite; a program needn't handle non-finite values.
Results may differ from the reference program's by a relative error of at most 0.014.
Values may be sent and summed in bfloat16 or wider, within the bound.
No kernel may reach another device: no remote copies, remote signals or barrier semaphores. Data moves between devices by JAX's collectives and lax.ppermute only.
A program may use at most 128 MiB of HBM per device.

```python
import jax
import jax.numpy as jnp
from jax import lax

D = 2048
FF = 1408
TOK_DEV = 128
BEAM = 4
EXPERTS = 64
DP_COPIES = 8
CANDIDATES = 512
REQUESTS = 128
TOKENS = 65536
CAP = 3
N_EXPERT = 64
N_DP = 8


def route_table(key):
    key = jax.random.fold_in(key, 101)
    key_a, key_b, key_c, key_d = jax.random.split(key, 4)
    blocks = TOKENS // TOK_DEV
    row_width = EXPERTS * CAP
    slot_index = jnp.arange(row_width, dtype=jnp.int32)
    slot_owner = slot_index // CAP
    jitter = jax.random.randint(key_a, (blocks, row_width), 0, 4096)
    favour = jax.random.randint(key_b, (EXPERTS,), 0, 4096)
    hottest = jax.random.randint(key_c, (), 0, EXPERTS)
    priority = jitter + favour[slot_owner] + jnp.where(slot_owner == hottest, 8192, 0)
    keyed_score = priority * row_width + slot_index
    ranking = jnp.argsort(-keyed_score, axis=1, stable=True)[:, :TOK_DEV]
    chosen = (ranking // CAP).astype(jnp.int32)
    chosen = jax.random.permutation(key_d, chosen, axis=1, independent=True)
    return chosen.reshape(TOKENS, 1)


def request_order(key):
    return jax.random.permutation(jax.random.fold_in(key, 202), CANDIDATES)


def draw_expert_ids(key, part):
    return route_table(key).astype(jnp.int32)


def draw_log_grad(key, part):
    key = jax.random.fold_in(key, 13)
    values = jnp.clip(jax.random.normal(key, (TOKENS, D), jnp.float32), -6.0, 6.0)
    return values.astype(jnp.bfloat16)


def draw_router_logits(key, part):
    chosen = route_table(key)
    key = jax.random.fold_in(key, 7)
    key_a, key_b = jax.random.split(key, 2)
    columns = jnp.arange(EXPERTS, dtype=jnp.int32)[None, :]
    chosen_mark = (chosen == columns).astype(jnp.float32)
    jitter = 0.25 * jnp.clip(jax.random.normal(key_a, (TOKENS, EXPERTS), jnp.float32), -4.0, 4.0)
    boost = jax.random.uniform(key_b, (TOKENS, 1), jnp.float32, 1.6, 2.4)
    return jitter + chosen_mark * boost


def draw_request_ids(key, part):
    ranking = request_order(key)
    return (ranking // BEAM).astype(jnp.int32)


def draw_risk_points(key, part):
    ranking = request_order(key)
    key = jax.random.fold_in(key, 11)
    key_a, key_b = jax.random.split(key, 2)
    member = ranking // BEAM
    seat_rank = ranking % BEAM
    offset = jax.random.randint(key_a, (CANDIDATES,), 0, 1501)
    offset = jnp.where((member == 0) & (seat_rank < 2), 0, offset)
    flip = jax.random.randint(key_b, (REQUESTS,), 0, 2)
    low_side = (seat_rank + flip[member]) % 2 == 0
    return jnp.where(low_side, offset, 8000 - offset).astype(jnp.int32)


def draw_cand_scores(key, part):
    ranking = request_order(key)
    key = jax.random.fold_in(key, 3)
    key_a, key_b = jax.random.split(key, 2)
    member = ranking // BEAM
    centre = jax.random.uniform(key_a, (REQUESTS,), jnp.float32, -20.0, 0.0)
    jitter = 0.6 * jnp.clip(jax.random.normal(key_b, (CANDIDATES,), jnp.float32), -2.5, 2.5)
    return centre[member] + jitter


def block_levels(own_key, shape, shards, smallest, largest):
    factor_of = 1.0
    for position, parts in shards:
        steps = jax.random.uniform(jax.random.fold_in(jax.random.fold_in(own_key, 6), position), (parts,), jnp.float32, smallest / len(shards), largest / len(shards))
        factor_of = factor_of * jnp.repeat(jnp.exp(steps), shape[position] // parts).reshape((-1,) + (1,) * (len(shape) - 1 - position))
    return factor_of


def scatter_about(key, dims, deviation, most, pieces=(), kind=jnp.bfloat16):
    entries = jax.random.normal(key, dims, jnp.float32) * deviation
    if len(pieces) > 0:
        entries = block_levels(key, dims, pieces, -0.22, 0.18) * entries
    return jnp.clip(entries, min=-most, max=most).astype(kind)


def setup_inputs(seed: int = 0) -> dict:
    seeds = jax.random.split(jax.random.key(seed), 13)
    return {
        "layer_input": scatter_about(seeds[0], (TOKENS, D), 1.0, 6.0, ((0, 512),)),
        "log_grad": draw_log_grad(jax.random.fold_in(seeds[12], 71), 0),
        "router_logits": draw_router_logits(jax.random.fold_in(seeds[12], 71), 0),
        "expert_ids": draw_expert_ids(jax.random.fold_in(seeds[12], 71), 0),
        "router_weight": scatter_about(seeds[4], (EXPERTS, D), D ** -0.5, 0.125),
        "gate_weight": scatter_about(seeds[5], (EXPERTS, D, FF), D ** -0.5, 0.125, ((0, 64), (2, 8))),
        "up_weight": scatter_about(seeds[6], (EXPERTS, D, FF), D ** -0.5, 0.125, ((0, 64), (2, 8))),
        "down_weight": scatter_about(seeds[7], (EXPERTS, FF, D), FF ** -0.5, 0.15625, ((0, 64), (1, 8))),
        "saved_pre": scatter_about(seeds[8], (EXPERTS, EXPERTS, DP_COPIES, CAP, 2, FF), 1.0, 6.0, ((0, 64), (5, 8))),
        "request_ids": draw_request_ids(jax.random.fold_in(seeds[12], 71), 0),
        "risk_points": draw_risk_points(jax.random.fold_in(seeds[12], 71), 0),
        "cand_scores": draw_cand_scores(jax.random.fold_in(seeds[12], 71), 0),
    }


NEG = -1.0e30


def expert_pass(packed):
    rows_grad, saved_rows, gate_e, up_e, down_e = packed
    gate_pre = saved_rows[:, 0].astype(jnp.float32)
    up_pre = saved_rows[:, 1].astype(jnp.float32)
    down_grad = jnp.einsum('rd,gfd->rgf', rows_grad.astype(jnp.float32), down_e.astype(jnp.float32))
    sigmoid_a = jax.nn.sigmoid(gate_pre)
    silu_a = gate_pre * sigmoid_a
    gate_parts = jnp.sum(down_grad * (silu_a * up_pre), axis=2).astype(jnp.bfloat16)
    grad_a = (down_grad * up_pre * sigmoid_a * (1.0 + gate_pre * (1.0 - sigmoid_a))).astype(jnp.bfloat16)
    grad_b = (down_grad * silu_a).astype(jnp.bfloat16)
    partial_value = jnp.einsum('rgf,dgf->grd', grad_a.astype(jnp.float32), gate_e.astype(jnp.float32))
    partial_value = partial_value + jnp.einsum('rgf,dgf->grd', grad_b.astype(jnp.float32), up_e.astype(jnp.float32))
    partial_value = partial_value.astype(jnp.bfloat16)
    routed = jnp.sum(partial_value.astype(jnp.float32), axis=0).astype(jnp.bfloat16)
    gate_grad = jnp.sum(gate_parts.astype(jnp.float32), axis=1).astype(jnp.bfloat16)
    return routed, gate_grad


def reference(layer_input, log_grad, router_logits, expert_ids, router_weight, gate_weight, up_weight, down_weight, saved_pre, request_ids, risk_points, cand_scores):
    risk_value = risk_points.astype(jnp.float32) * 0.001
    member = request_ids[:, None] == jnp.arange(REQUESTS, dtype=jnp.int32)[None, :]
    peak_score = jnp.max(jnp.where(member, cand_scores[:, None], NEG), axis=0)
    lifted = jnp.exp(cand_scores - peak_score[request_ids])
    mass_sum = jnp.sum(jnp.where(member, lifted[:, None], 0.0), axis=0)
    loaded_sum = jnp.sum(jnp.where(member, (lifted * risk_value)[:, None], 0.0), axis=0)
    cand_prob = lifted / mass_sum[request_ids]
    cand_weight = cand_prob * (risk_value - loaded_sum[request_ids] / mass_sum[request_ids])
    token_weight = jnp.repeat(cand_weight, TOK_DEV)
    scaled = (token_weight[:, None] * log_grad.astype(jnp.float32)).astype(jnp.bfloat16)

    cand_count = N_EXPERT * N_DP
    chosen = expert_ids[:, 0].reshape(cand_count, TOK_DEV)
    one_hot = (chosen[:, :, None] == jnp.arange(EXPERTS, dtype=jnp.int32)[None, None, :]).astype(jnp.int32)
    slot_rank = jnp.sum(one_hot * (jnp.cumsum(one_hot, axis=1).astype(jnp.int32) - 1), axis=2).astype(jnp.int32)
    anchor = jnp.arange(cand_count, dtype=jnp.int32)[:, None]
    row_count = cand_count * CAP
    slot_index = (chosen * row_count + anchor * CAP + slot_rank).reshape(-1).astype(jnp.int32)

    buffer = jnp.zeros((EXPERTS * row_count, D), jnp.bfloat16).at[slot_index].set(scaled)
    buffer = buffer.reshape(EXPERTS, row_count, D)
    saved_rows = saved_pre.reshape(EXPERTS, row_count, 2, N_DP, FF // N_DP)
    gate_groups = gate_weight.reshape(EXPERTS, D, N_DP, FF // N_DP)
    up_groups = up_weight.reshape(EXPERTS, D, N_DP, FF // N_DP)
    down_groups = down_weight.reshape(EXPERTS, N_DP, FF // N_DP, D)
    routed, gate_grad = lax.map(expert_pass, (buffer, saved_rows, gate_groups, up_groups, down_groups))
    routed_tok = routed.reshape(EXPERTS * row_count, D)[slot_index].astype(jnp.float32)
    grad_tok = gate_grad.reshape(-1)[slot_index].astype(jnp.float32)

    chosen_mark = (expert_ids[:, 0][:, None] == jnp.arange(EXPERTS, dtype=jnp.int32)[None, :]).astype(jnp.float32)
    peak_logit = jnp.max(router_logits, axis=1, keepdims=True)
    expd = jnp.exp(router_logits - peak_logit)
    router_prob = expd / jnp.sum(expd, axis=1, keepdims=True)
    chosen_prob = jnp.sum(router_prob * chosen_mark, axis=1)
    logit_grad = ((grad_tok * chosen_prob)[:, None] * (chosen_mark - router_prob)).astype(jnp.bfloat16)
    input_grad = (chosen_prob[:, None] * routed_tok + jnp.dot(logit_grad, router_weight, preferred_element_type=jnp.float32)).astype(jnp.bfloat16)
    router_grad = jnp.dot(logit_grad.T, layer_input, preferred_element_type=jnp.float32)
    return input_grad, router_grad
```

```python
import jax
import jax.numpy as jnp
from jax import lax
from jax.sharding import PartitionSpec as P

NEG = -1e30


def local(
    layer_input,
    log_grad,
    router_logits,
    expert_ids,
    router_weight,
    gate_weight,
    up_weight,
    down_weight,
    saved_pre,
    request_ids,
    risk_points,
    cand_scores,
):
    expert_count = lax.axis_size("expert")
    dp_count = lax.axis_size("dp")
    experts = router_weight.shape[0]
    cap = saved_pre.shape[3]
    hidden = saved_pre.shape[5]
    width = layer_input.shape[1]
    rows = expert_count * cap
    f32, bf16 = jnp.float32, jnp.bfloat16

    down_full = lax.all_gather(down_weight[0], "dp", axis=0, tiled=True)

    chosen = expert_ids[:, 0]
    one_hot = (chosen[:, None] == jnp.arange(experts, dtype=jnp.int32)[None, :]).astype(jnp.int32)
    slot_rank = jnp.sum(one_hot * (jnp.cumsum(one_hot, axis=0) - 1), axis=1)
    target = chosen * cap + slot_rank
    placer = (jnp.arange(experts * cap, dtype=jnp.int32)[:, None] == target[None, :]).astype(bf16)
    outgoing = jnp.dot(placer, log_grad, preferred_element_type=f32).astype(bf16)
    expert_rows = lax.all_to_all(
        outgoing.reshape(experts, cap, width), "expert", split_axis=0, concat_axis=0, tiled=True
    )

    risk_value = risk_points[0].astype(f32) * 0.001
    lane = jnp.arange(128, dtype=jnp.int32)
    record = jnp.where(
        lane == 0,
        request_ids[0].astype(f32),
        jnp.where(lane == 1, cand_scores[0], jnp.where(lane == 2, risk_value, 0.0)),
    )
    records = jnp.broadcast_to(record[None, None, :], (expert_count, 1, 128))
    records = lax.all_to_all(records, "expert", split_axis=0, concat_axis=0, tiled=True)
    records = jnp.broadcast_to(records.reshape(1, expert_count, 128), (dp_count, expert_count, 128))
    records = lax.all_to_all(records, "dp", split_axis=0, concat_axis=0, tiled=True)
    expert_rows, records, down_full, saved_pre = lax.optimization_barrier(
        (expert_rows, records, down_full, saved_pre)
    )
    member = records[:, :, 0:1] == request_ids[0].astype(f32)
    scores = records[:, :, 1:2]
    peak = jnp.max(jnp.where(member, scores, NEG))
    lifted = jnp.where(member, jnp.exp(jnp.where(member, scores, NEG) - peak), 0.0)
    mass = jnp.sum(lifted)
    loaded = jnp.sum(lifted * records[:, :, 2:3])
    cand_weight = jnp.exp(cand_scores[0] - peak) / mass * (risk_value - loaded / mass)

    slot_rows = expert_rows.reshape(rows, width)
    down_grad = jnp.einsum("fd,rd->fr", down_full, slot_rows, preferred_element_type=f32)
    down_grad = down_grad.astype(bf16).reshape(dp_count, hidden, rows)
    down_grad = lax.all_to_all(down_grad, "dp", split_axis=0, concat_axis=0, tiled=True)
    down_grad = down_grad.astype(f32)

    saved = jnp.transpose(saved_pre[0], (3, 1, 4, 0, 2)).reshape(2, dp_count, hidden, rows)
    gate_pre = saved[0].astype(f32)
    up_pre = saved[1].astype(f32)
    sigmoid_a = jax.nn.sigmoid(gate_pre)
    silu_a = gate_pre * sigmoid_a
    gate_parts = jnp.sum(down_grad * (silu_a * up_pre), axis=1)
    grad_a = (down_grad * up_pre * sigmoid_a * (1.0 + gate_pre * (1.0 - sigmoid_a))).astype(bf16)
    grad_b = (down_grad * silu_a).astype(bf16)
    part = jnp.einsum("zfr,df->zrd", grad_a, gate_weight[0], preferred_element_type=f32)
    part = part + jnp.einsum("zfr,df->zrd", grad_b, up_weight[0], preferred_element_type=f32)
    part = part.astype(bf16).reshape(dp_count * rows, width)
    routed = lax.psum_scatter(part, "dp", scatter_dimension=0, tiled=True)

    gate_sum = lax.all_to_all(gate_parts, "dp", split_axis=0, concat_axis=0, tiled=True)
    gate_sum = jnp.sum(gate_sum, axis=0).reshape(expert_count, 1, cap)
    home_grad = lax.all_to_all(gate_sum, "expert", split_axis=0, concat_axis=0, tiled=True)
    home_grad = home_grad.reshape(rows).astype(bf16)
    grad_tok = jnp.einsum("st,s->t", placer, home_grad, preferred_element_type=f32)

    chosen_mark = one_hot.astype(f32)
    peak_logit = jnp.max(router_logits, axis=1, keepdims=True)
    expd = jnp.exp(router_logits - peak_logit)
    router_prob = expd / jnp.sum(expd, axis=1, keepdims=True)
    chosen_prob = jnp.sum(router_prob * chosen_mark, axis=1) * cand_weight
    logit_grad = ((grad_tok * chosen_prob)[:, None] * (chosen_mark - router_prob)).astype(bf16)

    router_part = jnp.einsum("td,te->de", layer_input, logit_grad, preferred_element_type=f32)
    share = width // expert_count
    router_part = router_part.reshape(expert_count, share, experts)
    router_part = lax.all_to_all(router_part, "expert", split_axis=0, concat_axis=0, tiled=True)
    router_part = jnp.sum(router_part, axis=0).reshape(dp_count, share // dp_count, experts)
    router_part = lax.all_to_all(router_part, "dp", split_axis=0, concat_axis=0, tiled=True)
    router_grad = jnp.sum(router_part, axis=0).T

    homeward = lax.all_to_all(
        routed.reshape(expert_count, cap, width), "expert", split_axis=0, concat_axis=0, tiled=True
    )
    routed_tok = jnp.einsum(
        "st,sd->td", placer, homeward.reshape(rows, width), preferred_element_type=f32
    )
    input_grad = (
        chosen_prob[:, None] * routed_tok
        + jnp.dot(logit_grad, router_weight, preferred_element_type=f32)
    ).astype(bf16)
    return (input_grad, router_grad)


def solution(mesh):
    return jax.shard_map(
        local,
        mesh=mesh,
        in_specs=(
            P(("expert", "dp"), None),
            P(("expert", "dp"), None),
            P(("expert", "dp"), None),
            P(("expert", "dp"), None),
            P(),
            P("expert", None, "dp"),
            P("expert", None, "dp"),
            P("expert", "dp", None),
            P("expert", None, None, None, None, "dp"),
            P(("expert", "dp")),
            P(("expert", "dp")),
            P(("expert", "dp")),
        ),
        out_specs=(P(("expert", "dp"), None), P(None, ("expert", "dp"))),
        check_vma=False,
    )
```

```python
import jax
import jax.numpy as jnp
from jax import lax
from jax.experimental import pallas as pl
from jax.experimental.pallas import tpu as pltpu
from jax.sharding import PartitionSpec as P

NEG = -1e30
LANES = 128
RECORD_ROWS = 8


def nt_dot(left, right):
    return lax.dot_general(left, right, (((1,), (1,)), ((), ())), preferred_element_type=jnp.float32)


def tn_dot(left, right):
    return lax.dot_general(left, right, (((0,), (0,)), ((), ())), preferred_element_type=jnp.float32)


def down_kernel(down_ref, rows_ref, record_ref, out_ref):
    hidden = down_ref.shape[0]
    half = hidden // 2
    rows = rows_ref.shape[0]
    bf16 = jnp.bfloat16
    full = nt_dot(down_ref[...], rows_ref[...])
    head = full[:, :LANES]
    tail = full[:, LANES:]
    tail = jnp.concatenate([tail[:half], tail[half:]], axis=1)
    pick = (
        lax.broadcasted_iota(jnp.int32, (RECORD_ROWS, LANES), 0)
        == lax.broadcasted_iota(jnp.int32, (RECORD_ROWS, LANES), 1)
    ).astype(bf16)
    record = nt_dot(pick, record_ref[...])
    record = jnp.concatenate([record, jnp.zeros_like(record)], axis=1)
    out_ref[0, :hidden, :] = head.astype(bf16)
    out_ref[0, hidden:, :] = jnp.concatenate([tail, record], axis=0).astype(bf16)


def up_kernel(packed_ref, scale_a_ref, scale_b_ref, scale_g_ref, gate_ref, up_ref, part_ref, gate_part_ref):
    hidden = gate_ref.shape[0]
    half = hidden // 2
    bf16 = jnp.bfloat16
    head = packed_ref[0, :hidden, :].astype(jnp.float32)
    tail = packed_ref[0, hidden:, :].astype(jnp.float32)[:half]
    side = LANES // 2
    tail = jnp.concatenate([tail[:, :side], tail[:, side:]], axis=0)
    down_grad = jnp.concatenate([head, tail], axis=1)
    gate_part_ref[0] = jnp.sum(down_grad * scale_g_ref[0], axis=0, keepdims=True)
    grad_a = (down_grad * scale_a_ref[0]).astype(bf16)
    grad_b = (down_grad * scale_b_ref[0]).astype(bf16)
    part_ref[0] = (tn_dot(grad_a, gate_ref[...]) + tn_dot(grad_b, up_ref[...])).astype(bf16)


def local(
    layer_input,
    log_grad,
    router_logits,
    expert_ids,
    router_weight,
    gate_weight,
    up_weight,
    down_weight,
    saved_pre,
    request_ids,
    risk_points,
    cand_scores,
):
    expert_count = lax.axis_size("expert")
    dp_count = lax.axis_size("dp")
    experts = router_weight.shape[0]
    cap = saved_pre.shape[3]
    hidden = saved_pre.shape[5]
    width = layer_input.shape[1]
    rows = expert_count * cap
    packed_rows = hidden + hidden // 2 + RECORD_ROWS
    f32, bf16 = jnp.float32, jnp.bfloat16

    down_full = lax.all_gather(down_weight[0], "dp", axis=0, tiled=True)

    score = cand_scores[0]
    score_hi = lax.reduce_precision(score, 8, 7)
    score_mid = lax.reduce_precision(score - score_hi, 8, 7)
    score_lo = lax.reduce_precision(score - score_hi - score_mid, 8, 7)
    points = risk_points[0]
    pieces = (
        request_ids[0].astype(f32),
        score_hi,
        score_mid,
        score_lo,
        (points // 128).astype(f32),
        (points % 128).astype(f32),
    )
    lane = jnp.arange(width, dtype=jnp.int32)
    record = jnp.zeros((width,), f32)
    for place, piece in enumerate(pieces):
        record = jnp.where(lane == place, piece, record)

    chosen = expert_ids[:, 0]
    one_hot = (chosen[:, None] == jnp.arange(experts, dtype=jnp.int32)[None, :]).astype(jnp.int32)
    slot_rank = jnp.sum(one_hot * (jnp.cumsum(one_hot, axis=0) - 1), axis=1)
    line = jnp.arange(experts * (cap + 1), dtype=jnp.int32)
    spread = (line[:, None] == (chosen * (cap + 1) + slot_rank)[None, :]).astype(bf16)
    outgoing = jnp.dot(spread, log_grad, preferred_element_type=f32)
    outgoing = jnp.where((line % (cap + 1) == cap)[:, None], record[None, :], outgoing)
    outgoing = outgoing.astype(bf16).reshape(experts, cap + 1, width)
    arrived = lax.all_to_all(outgoing, "expert", split_axis=0, concat_axis=0, tiled=True)
    slot_rows = arrived[:, :cap].reshape(rows, width)
    record_rows = arrived[:, cap, :LANES]

    saved = jnp.transpose(saved_pre[0], (3, 1, 4, 0, 2)).reshape(2, dp_count, hidden, rows)
    gate_pre = saved[0].astype(f32)
    up_pre = saved[1].astype(f32)
    sigmoid_a = jax.nn.sigmoid(gate_pre)
    scale_b = gate_pre * sigmoid_a
    scale_g = scale_b * up_pre
    scale_a = up_pre * sigmoid_a * (1.0 + gate_pre * (1.0 - sigmoid_a))
    slot_rows, record_rows, scale_a, scale_b, scale_g, down_full = lax.optimization_barrier(
        (slot_rows, record_rows, scale_a, scale_b, scale_g, down_full)
    )

    packed = pl.pallas_call(
        down_kernel,
        grid=(dp_count,),
        in_specs=[
            pl.BlockSpec((hidden, width), lambda i: (i, 0)),
            pl.BlockSpec((rows, width), lambda i: (0, 0)),
            pl.BlockSpec((expert_count, LANES), lambda i: (0, 0)),
        ],
        out_specs=pl.BlockSpec((1, packed_rows, LANES), lambda i: (i, 0, 0)),
        out_shape=jax.ShapeDtypeStruct((dp_count, packed_rows, LANES), bf16),
        compiler_params=pltpu.CompilerParams(vmem_limit_bytes=32 * 2**20),
        cost_estimate=pl.CostEstimate(
            flops=2 * rows * width * hidden * dp_count,
            bytes_accessed=2 * width * hidden * dp_count,
            transcendentals=0,
        ),
    )(down_full, slot_rows, record_rows)
    packed = lax.all_to_all(packed, "dp", split_axis=0, concat_axis=0, tiled=True)

    part, gate_parts = pl.pallas_call(
        up_kernel,
        grid=(dp_count,),
        in_specs=[
            pl.BlockSpec((1, packed_rows, LANES), lambda i: (i, 0, 0)),
            pl.BlockSpec((1, hidden, rows), lambda i: (i, 0, 0)),
            pl.BlockSpec((1, hidden, rows), lambda i: (i, 0, 0)),
            pl.BlockSpec((1, hidden, rows), lambda i: (i, 0, 0)),
            pl.BlockSpec((hidden, width), lambda i: (0, 0)),
            pl.BlockSpec((hidden, width), lambda i: (0, 0)),
        ],
        out_specs=[
            pl.BlockSpec((1, rows, width), lambda i: (i, 0, 0)),
            pl.BlockSpec((1, 1, rows), lambda i: (i, 0, 0)),
        ],
        out_shape=[
            jax.ShapeDtypeStruct((dp_count, rows, width), bf16),
            jax.ShapeDtypeStruct((dp_count, 1, rows), f32),
        ],
        compiler_params=pltpu.CompilerParams(vmem_limit_bytes=32 * 2**20),
        cost_estimate=pl.CostEstimate(
            flops=4 * rows * width * hidden * dp_count,
            bytes_accessed=2 * rows * width * dp_count,
            transcendentals=0,
        ),
    )(packed, scale_a, scale_b, scale_g, gate_weight[0].T, up_weight[0].T)
    routed = lax.psum_scatter(
        part.reshape(dp_count * rows, width), "dp", scatter_dimension=0, tiled=True
    )

    records = packed[:, hidden + hidden // 2 :, :expert_count].astype(f32)
    member = records[:, 0] == pieces[0]
    scores = jnp.where(member, records[:, 1] + records[:, 2] + records[:, 3], NEG)
    risks = (records[:, 4] * 128.0 + records[:, 5]) * 0.001
    peak = jnp.max(scores)
    lifted = jnp.where(member, jnp.exp(scores - peak), 0.0)
    mass = jnp.sum(lifted)
    loaded = jnp.sum(lifted * risks)
    risk_value = points.astype(f32) * 0.001
    cand_weight = jnp.exp(score - peak) / mass * (risk_value - loaded / mass)

    gate_sum = lax.all_to_all(gate_parts, "dp", split_axis=0, concat_axis=0, tiled=True)
    gate_sum = jnp.sum(gate_sum, axis=0).reshape(expert_count, 1, cap)
    home_grad = lax.all_to_all(gate_sum, "expert", split_axis=0, concat_axis=0, tiled=True)
    home_grad = home_grad.reshape(rows).astype(bf16)
    placer = (
        jnp.arange(rows, dtype=jnp.int32)[:, None] == (chosen * cap + slot_rank)[None, :]
    ).astype(bf16)
    grad_tok = jnp.einsum("st,s->t", placer, home_grad, preferred_element_type=f32)

    chosen_mark = one_hot.astype(f32)
    peak_logit = jnp.max(router_logits, axis=1, keepdims=True)
    expd = jnp.exp(router_logits - peak_logit)
    router_prob = expd / jnp.sum(expd, axis=1, keepdims=True)
    chosen_prob = jnp.sum(router_prob * chosen_mark, axis=1) * cand_weight
    logit_grad = ((grad_tok * chosen_prob)[:, None] * (chosen_mark - router_prob)).astype(bf16)

    router_part = jnp.einsum("td,te->de", layer_input, logit_grad, preferred_element_type=f32)
    share = width // expert_count
    router_part = router_part.reshape(expert_count, share, experts)
    router_part = lax.all_to_all(router_part, "expert", split_axis=0, concat_axis=0, tiled=True)
    router_part = jnp.sum(router_part, axis=0).reshape(dp_count, share // dp_count, experts)
    router_part = lax.all_to_all(router_part, "dp", split_axis=0, concat_axis=0, tiled=True)
    router_grad = jnp.sum(router_part, axis=0).T

    homeward = lax.all_to_all(
        routed.reshape(expert_count, rows * width // expert_count // LANES, LANES),
        "expert",
        split_axis=0,
        concat_axis=0,
        tiled=True,
    )
    routed_tok = jnp.einsum(
        "st,sd->td", placer, homeward.reshape(rows, width), preferred_element_type=f32
    )
    input_grad = (
        chosen_prob[:, None] * routed_tok
        + jnp.dot(logit_grad, router_weight, preferred_element_type=f32)
    ).astype(bf16)
    return (input_grad, router_grad)


def solution(mesh):
    return jax.shard_map(
        local,
        mesh=mesh,
        in_specs=(
            P(("expert", "dp"), None),
            P(("expert", "dp"), None),
            P(("expert", "dp"), None),
            P(("expert", "dp"), None),
            P(),
            P("expert", None, "dp"),
            P("expert", None, "dp"),
            P("expert", "dp", None),
            P("expert", None, None, None, None, "dp"),
            P(("expert", "dp")),
            P(("expert", "dp")),
            P(("expert", "dp")),
        ),
        out_specs=(P(("expert", "dp"), None), P(None, ("expert", "dp"))),
        check_vma=False,
    )
```

```python
import functools

import jax
import jax.numpy as jnp
from jax import lax
from jax.experimental import pallas as pl
from jax.experimental.pallas import tpu as pltpu
from jax.sharding import PartitionSpec as P

NEG = -1e30
LANES = 128
RECORD_ROWS = 8
DOWN_PIECES = 4
DOWN_HOLDERS = 4
UP_SENDERS = 2
UP_CHUNKS = 4
VMEM_GRANT = 32 * 2**20


def nt_dot(left, right):
    return lax.dot_general(left, right, (((1,), (1,)), ((), ())), preferred_element_type=jnp.float32)


def down_kernel(*refs):
    *down_refs, rows_ref, record_ref, out_ref = refs
    holders = out_ref.shape[0]
    hidden = down_refs[0].shape[0] // holders
    half = hidden // 2
    span = down_refs[0].shape[1]
    bf16 = jnp.bfloat16
    full = sum(
        nt_dot(ref[...], rows_ref[:, place * span : (place + 1) * span])
        for place, ref in enumerate(down_refs)
    )
    pick = (
        lax.broadcasted_iota(jnp.int32, (RECORD_ROWS, LANES), 0)
        == lax.broadcasted_iota(jnp.int32, (RECORD_ROWS, LANES), 1)
    ).astype(bf16)
    record = nt_dot(pick, record_ref[...])
    record = jnp.concatenate([record, jnp.zeros_like(record)], axis=1)
    for holder in range(holders):
        block = full[holder * hidden : (holder + 1) * hidden]
        tail = block[:, LANES:]
        tail = jnp.concatenate([tail[:half], tail[half:]], axis=1)
        out_ref[holder, :hidden, :] = block[:, :LANES].astype(bf16)
        out_ref[holder, hidden:, :] = jnp.concatenate([tail, record], axis=0).astype(bf16)


def up_kernel(
    packed_ref, scale_a_ref, scale_b_ref, scale_g_ref, gate_ref, up_ref, part_ref, gate_part_ref
):
    senders = packed_ref.shape[0]
    hidden, width = gate_ref.shape
    half = hidden // 2
    seam = LANES // 2
    span = width // UP_CHUNKS
    f32, bf16 = jnp.float32, jnp.bfloat16
    for sender in range(senders):
        head = packed_ref[sender, :hidden, :].astype(f32)
        tail = packed_ref[sender, hidden:, :].astype(f32)[:half]
        tail = jnp.concatenate([tail[:, :seam], tail[:, seam:]], axis=0)
        down_grad = jnp.concatenate([head, tail], axis=1)
        gate_part_ref[sender] = jnp.sum(down_grad * scale_g_ref[sender], axis=0, keepdims=True)
        grad_a = jnp.transpose(down_grad * scale_a_ref[sender]).astype(bf16)
        grad_b = jnp.transpose(down_grad * scale_b_ref[sender]).astype(bf16)
        for chunk in range(UP_CHUNKS):
            columns = slice(chunk * span, (chunk + 1) * span)
            part = jnp.dot(grad_a, gate_ref[:, columns], preferred_element_type=f32)
            part = part + jnp.dot(grad_b, up_ref[:, columns], preferred_element_type=f32)
            part_ref[sender, :, columns] = part.astype(bf16)


def piece_index(place, i):
    return (i, place)


def local(
    layer_input,
    log_grad,
    router_logits,
    expert_ids,
    router_weight,
    gate_weight,
    up_weight,
    down_weight,
    saved_pre,
    request_ids,
    risk_points,
    cand_scores,
):
    expert_count = lax.axis_size("expert")
    dp_count = lax.axis_size("dp")
    experts = router_weight.shape[0]
    cap = saved_pre.shape[3]
    hidden = saved_pre.shape[5]
    width = layer_input.shape[1]
    rows = expert_count * cap
    packed_rows = hidden + hidden // 2 + RECORD_ROWS
    f32, bf16 = jnp.float32, jnp.bfloat16

    down_full = lax.all_gather(down_weight[0], "dp", axis=0, tiled=True)

    score = cand_scores[0]
    score_hi = lax.reduce_precision(score, 8, 7)
    score_mid = lax.reduce_precision(score - score_hi, 8, 7)
    score_lo = lax.reduce_precision(score - score_hi - score_mid, 8, 7)
    points = risk_points[0]
    pieces = (
        request_ids[0].astype(f32),
        score_hi,
        score_mid,
        score_lo,
        (points // 128).astype(f32),
        (points % 128).astype(f32),
    )
    lane = jnp.arange(width, dtype=jnp.int32)
    record = jnp.zeros((width,), f32)
    for place, piece in enumerate(pieces):
        record = jnp.where(lane == place, piece, record)

    chosen = expert_ids[:, 0]
    one_hot = (chosen[:, None] == jnp.arange(experts, dtype=jnp.int32)[None, :]).astype(jnp.int32)
    slot_rank = jnp.sum(one_hot * (jnp.cumsum(one_hot, axis=0) - 1), axis=1)
    line = jnp.arange(experts * (cap + 1), dtype=jnp.int32)
    spread = (line[:, None] == (chosen * (cap + 1) + slot_rank)[None, :]).astype(bf16)
    outgoing = jnp.dot(spread, log_grad, preferred_element_type=f32)
    outgoing = jnp.where((line % (cap + 1) == cap)[:, None], record[None, :], outgoing)
    outgoing = outgoing.astype(bf16).reshape(experts, cap + 1, width)
    arrived = lax.all_to_all(outgoing, "expert", split_axis=0, concat_axis=0, tiled=True)
    slot_rows = arrived[:, :cap].reshape(rows, width)
    record_rows = arrived[:, cap, :LANES]

    saved = jnp.transpose(saved_pre[0], (3, 1, 4, 0, 2)).reshape(2, dp_count, hidden, rows)
    gate_pre = saved[0].astype(f32)
    up_pre = saved[1].astype(f32)
    sigmoid_a = jax.nn.sigmoid(gate_pre)
    scale_b = gate_pre * sigmoid_a
    scale_g = scale_b * up_pre
    scale_a = up_pre * sigmoid_a * (1.0 + gate_pre * (1.0 - sigmoid_a))
    slot_rows, record_rows, scale_a, scale_b, scale_g, down_full = lax.optimization_barrier(
        (slot_rows, record_rows, scale_a, scale_b, scale_g, down_full)
    )

    span = width // DOWN_PIECES
    packed = pl.pallas_call(
        down_kernel,
        grid=(dp_count // DOWN_HOLDERS,),
        in_specs=[
            pl.BlockSpec((DOWN_HOLDERS * hidden, span), functools.partial(piece_index, place))
            for place in range(DOWN_PIECES)
        ]
        + [
            pl.BlockSpec((rows, width), lambda i: (0, 0)),
            pl.BlockSpec((expert_count, LANES), lambda i: (0, 0)),
        ],
        out_specs=pl.BlockSpec((DOWN_HOLDERS, packed_rows, LANES), lambda i: (i, 0, 0)),
        out_shape=jax.ShapeDtypeStruct((dp_count, packed_rows, LANES), bf16),
        compiler_params=pltpu.CompilerParams(vmem_limit_bytes=VMEM_GRANT),
        cost_estimate=pl.CostEstimate(
            flops=2 * rows * width * hidden * dp_count,
            bytes_accessed=2 * width * hidden * dp_count,
            transcendentals=0,
        ),
    )(
        *[pltpu.with_memory_space_constraint(down_full, pltpu.HBM)] * DOWN_PIECES,
        slot_rows,
        record_rows,
    )
    packed = lax.all_to_all(packed, "dp", split_axis=0, concat_axis=0, tiled=True)

    part, gate_parts = pl.pallas_call(
        up_kernel,
        grid=(dp_count // UP_SENDERS,),
        in_specs=[
            pl.BlockSpec((UP_SENDERS, packed_rows, LANES), lambda i: (i, 0, 0)),
            pl.BlockSpec((UP_SENDERS, hidden, rows), lambda i: (i, 0, 0)),
            pl.BlockSpec((UP_SENDERS, hidden, rows), lambda i: (i, 0, 0)),
            pl.BlockSpec((UP_SENDERS, hidden, rows), lambda i: (i, 0, 0)),
            pl.BlockSpec((hidden, width), lambda i: (0, 0)),
            pl.BlockSpec((hidden, width), lambda i: (0, 0)),
        ],
        out_specs=[
            pl.BlockSpec((UP_SENDERS, rows, width), lambda i: (i, 0, 0)),
            pl.BlockSpec((UP_SENDERS, 1, rows), lambda i: (i, 0, 0)),
        ],
        out_shape=[
            pltpu.HBM((dp_count, rows, width), bf16),
            jax.ShapeDtypeStruct((dp_count, 1, rows), f32),
        ],
        compiler_params=pltpu.CompilerParams(vmem_limit_bytes=VMEM_GRANT),
        cost_estimate=pl.CostEstimate(
            flops=4 * rows * width * hidden * dp_count,
            bytes_accessed=2 * rows * width * dp_count,
            transcendentals=0,
        ),
    )(packed, scale_a, scale_b, scale_g, gate_weight[0].T, up_weight[0].T)
    routed = lax.psum_scatter(
        part.reshape(dp_count * rows, width), "dp", scatter_dimension=0, tiled=True
    )

    records = packed[:, hidden + hidden // 2 :, :expert_count].astype(f32)
    member = records[:, 0] == pieces[0]
    scores = jnp.where(member, records[:, 1] + records[:, 2] + records[:, 3], NEG)
    risks = (records[:, 4] * 128.0 + records[:, 5]) * 0.001
    peak = jnp.max(scores)
    lifted = jnp.where(member, jnp.exp(scores - peak), 0.0)
    mass = jnp.sum(lifted)
    loaded = jnp.sum(lifted * risks)
    risk_value = points.astype(f32) * 0.001
    cand_weight = jnp.exp(score - peak) / mass * (risk_value - loaded / mass)

    gate_sum = lax.all_to_all(gate_parts, "dp", split_axis=0, concat_axis=0, tiled=True)
    gate_sum = jnp.sum(gate_sum, axis=0).reshape(expert_count, 1, cap)
    home_grad = lax.all_to_all(gate_sum, "expert", split_axis=0, concat_axis=0, tiled=True)
    home_grad = home_grad.reshape(rows).astype(bf16)
    placer = (
        jnp.arange(rows, dtype=jnp.int32)[:, None] == (chosen * cap + slot_rank)[None, :]
    ).astype(bf16)
    grad_tok = jnp.einsum("st,s->t", placer, home_grad, preferred_element_type=f32)

    chosen_mark = one_hot.astype(f32)
    peak_logit = jnp.max(router_logits, axis=1, keepdims=True)
    expd = jnp.exp(router_logits - peak_logit)
    router_prob = expd / jnp.sum(expd, axis=1, keepdims=True)
    chosen_prob = jnp.sum(router_prob * chosen_mark, axis=1) * cand_weight
    logit_grad = ((grad_tok * chosen_prob)[:, None] * (chosen_mark - router_prob)).astype(bf16)

    router_part = jnp.einsum("td,te->de", layer_input, logit_grad, preferred_element_type=f32)
    share = width // expert_count
    router_part = router_part.reshape(expert_count, share, experts)
    router_part = lax.all_to_all(router_part, "expert", split_axis=0, concat_axis=0, tiled=True)
    router_part = jnp.sum(router_part, axis=0).reshape(dp_count, share // dp_count, experts)
    router_part = lax.all_to_all(router_part, "dp", split_axis=0, concat_axis=0, tiled=True)
    router_grad = jnp.sum(router_part, axis=0).T

    routed, router_grad = lax.optimization_barrier((routed, router_grad))
    homeward = lax.all_to_all(
        routed.reshape(expert_count, rows * width // expert_count // LANES, LANES),
        "expert",
        split_axis=0,
        concat_axis=0,
        tiled=True,
    )
    routed_tok = jnp.einsum(
        "st,sd->td", placer, homeward.reshape(rows, width), preferred_element_type=f32
    )
    input_grad = (
        chosen_prob[:, None] * routed_tok
        + jnp.dot(logit_grad, router_weight, preferred_element_type=f32)
    ).astype(bf16)
    return (input_grad, router_grad)


def solution(mesh):
    return jax.shard_map(
        local,
        mesh=mesh,
        in_specs=(
            P(("expert", "dp"), None),
            P(("expert", "dp"), None),
            P(("expert", "dp"), None),
            P(("expert", "dp"), None),
            P(),
            P("expert", None, "dp"),
            P("expert", None, "dp"),
            P("expert", "dp", None),
            P("expert", None, None, None, None, "dp"),
            P(("expert", "dp")),
            P(("expert", "dp")),
            P(("expert", "dp")),
        ),
        out_specs=(P(("expert", "dp"), None), P(None, ("expert", "dp"))),
        check_vma=False,
    )
```

```python
import functools

import jax
import jax.numpy as jnp
from jax import lax
from jax.experimental import pallas as pl
from jax.experimental.pallas import tpu as pltpu
from jax.sharding import PartitionSpec as P

NEG = -1e30
LANES = 128
RECORD_ROWS = 8
DOWN_PIECES = 4
DOWN_HOLDERS = 4
UP_SENDERS = 2
UP_CHUNKS = 4
VMEM_GRANT = 32 * 2**20


def nt_dot(left, right):
    return lax.dot_general(left, right, (((1,), (1,)), ((), ())), preferred_element_type=jnp.float32)


def down_kernel(*refs):
    *down_refs, rows_ref, record_ref, out_ref = refs
    holders = out_ref.shape[0]
    hidden = down_refs[0].shape[0] // holders
    half = hidden // 2
    span = down_refs[0].shape[1]
    bf16 = jnp.bfloat16
    full = sum(
        nt_dot(ref[...], rows_ref[:, place * span : (place + 1) * span])
        for place, ref in enumerate(down_refs)
    )
    pick = (
        lax.broadcasted_iota(jnp.int32, (RECORD_ROWS, LANES), 0)
        == lax.broadcasted_iota(jnp.int32, (RECORD_ROWS, LANES), 1)
    ).astype(bf16)
    record = nt_dot(pick, record_ref[...])
    record = jnp.concatenate([record, jnp.zeros_like(record)], axis=1)
    for holder in range(holders):
        block = full[holder * hidden : (holder + 1) * hidden]
        tail = block[:, LANES:]
        tail = jnp.concatenate([tail[:half], tail[half:]], axis=1)
        out_ref[holder, :hidden, :] = block[:, :LANES].astype(bf16)
        out_ref[holder, hidden:, :] = jnp.concatenate([tail, record], axis=0).astype(bf16)


def up_kernel(
    packed_ref, scale_a_ref, scale_b_ref, scale_g_ref, gate_ref, up_ref, part_ref, gate_part_ref
):
    senders = packed_ref.shape[0]
    hidden, width = gate_ref.shape
    half = hidden // 2
    seam = LANES // 2
    span = width // UP_CHUNKS
    f32, bf16 = jnp.float32, jnp.bfloat16
    for sender in range(senders):
        head = packed_ref[sender, :hidden, :].astype(f32)
        tail = packed_ref[sender, hidden:, :].astype(f32)[:half]
        tail = jnp.concatenate([tail[:, :seam], tail[:, seam:]], axis=0)
        down_grad = jnp.concatenate([head, tail], axis=1)
        gate_part_ref[sender] = jnp.sum(down_grad * scale_g_ref[sender], axis=0, keepdims=True)
        grad_a = jnp.transpose(down_grad * scale_a_ref[sender]).astype(bf16)
        grad_b = jnp.transpose(down_grad * scale_b_ref[sender]).astype(bf16)
        for chunk in range(UP_CHUNKS):
            columns = slice(chunk * span, (chunk + 1) * span)
            part = jnp.dot(grad_a, gate_ref[:, columns], preferred_element_type=f32)
            part = part + jnp.dot(grad_b, up_ref[:, columns], preferred_element_type=f32)
            part_ref[sender, :, columns] = part.astype(bf16)


def piece_index(place, i):
    return (i, place)


def local(
    layer_input,
    log_grad,
    router_logits,
    expert_ids,
    router_weight,
    gate_weight,
    up_weight,
    down_weight,
    saved_pre,
    request_ids,
    risk_points,
    cand_scores,
):
    expert_count = lax.axis_size("expert")
    dp_count = lax.axis_size("dp")
    experts = router_weight.shape[0]
    cap = saved_pre.shape[3]
    hidden = saved_pre.shape[5]
    width = layer_input.shape[1]
    rows = expert_count * cap
    packed_rows = hidden + hidden // 2 + RECORD_ROWS
    f32, bf16 = jnp.float32, jnp.bfloat16

    down_full = lax.all_gather(down_weight[0], "dp", axis=0, tiled=True)

    score = cand_scores[0]
    score_hi = lax.reduce_precision(score, 8, 7)
    score_mid = lax.reduce_precision(score - score_hi, 8, 7)
    score_lo = lax.reduce_precision(score - score_hi - score_mid, 8, 7)
    points = risk_points[0]
    pieces = (
        request_ids[0].astype(f32),
        score_hi,
        score_mid,
        score_lo,
        (points // 128).astype(f32),
        (points % 128).astype(f32),
    )
    lane = jnp.arange(width, dtype=jnp.int32)
    record = jnp.zeros((width,), f32)
    for place, piece in enumerate(pieces):
        record = jnp.where(lane == place, piece, record)

    chosen = expert_ids[:, 0]
    one_hot = (chosen[:, None] == jnp.arange(experts, dtype=jnp.int32)[None, :]).astype(jnp.int32)
    slot_rank = jnp.sum(one_hot * (jnp.cumsum(one_hot, axis=0) - 1), axis=1)
    line = jnp.arange(experts * (cap + 1), dtype=jnp.int32)
    spread = (line[:, None] == (chosen * (cap + 1) + slot_rank)[None, :]).astype(bf16)
    outgoing = jnp.dot(spread, log_grad, preferred_element_type=f32)
    outgoing = jnp.where((line % (cap + 1) == cap)[:, None], record[None, :], outgoing)
    outgoing = outgoing.astype(bf16).reshape(experts, cap + 1, width)
    arrived = lax.all_to_all(outgoing, "expert", split_axis=0, concat_axis=0, tiled=True)
    slot_rows = arrived[:, :cap].reshape(rows, width)
    record_rows = arrived[:, cap, :LANES]

    saved = jnp.transpose(saved_pre[0], (3, 1, 4, 0, 2)).reshape(2, dp_count, hidden, rows)
    gate_pre = saved[0].astype(f32)
    up_pre = saved[1].astype(f32)
    sigmoid_a = jax.nn.sigmoid(gate_pre)
    scale_b = gate_pre * sigmoid_a
    scale_g = scale_b * up_pre
    scale_a = up_pre * sigmoid_a * (1.0 + gate_pre * (1.0 - sigmoid_a))
    slot_rows, record_rows, scale_a, scale_b, scale_g, down_full = lax.optimization_barrier(
        (slot_rows, record_rows, scale_a, scale_b, scale_g, down_full)
    )

    span = width // DOWN_PIECES
    packed = pl.pallas_call(
        down_kernel,
        grid=(dp_count // DOWN_HOLDERS,),
        in_specs=[
            pl.BlockSpec((DOWN_HOLDERS * hidden, span), functools.partial(piece_index, place))
            for place in range(DOWN_PIECES)
        ]
        + [
            pl.BlockSpec((rows, width), lambda i: (0, 0)),
            pl.BlockSpec((expert_count, LANES), lambda i: (0, 0)),
        ],
        out_specs=pl.BlockSpec((DOWN_HOLDERS, packed_rows, LANES), lambda i: (i, 0, 0)),
        out_shape=jax.ShapeDtypeStruct((dp_count, packed_rows, LANES), bf16),
        compiler_params=pltpu.CompilerParams(vmem_limit_bytes=VMEM_GRANT),
        cost_estimate=pl.CostEstimate(
            flops=2 * rows * width * hidden * dp_count,
            bytes_accessed=2 * width * hidden * dp_count,
            transcendentals=0,
        ),
    )(
        *[pltpu.with_memory_space_constraint(down_full, pltpu.HBM)] * DOWN_PIECES,
        slot_rows,
        record_rows,
    )
    packed = lax.all_to_all(packed, "dp", split_axis=0, concat_axis=0, tiled=True)

    part, gate_parts = pl.pallas_call(
        up_kernel,
        grid=(dp_count // UP_SENDERS,),
        in_specs=[
            pl.BlockSpec((UP_SENDERS, packed_rows, LANES), lambda i: (i, 0, 0)),
            pl.BlockSpec((UP_SENDERS, hidden, rows), lambda i: (i, 0, 0)),
            pl.BlockSpec((UP_SENDERS, hidden, rows), lambda i: (i, 0, 0)),
            pl.BlockSpec((UP_SENDERS, hidden, rows), lambda i: (i, 0, 0)),
            pl.BlockSpec((hidden, width), lambda i: (0, 0)),
            pl.BlockSpec((hidden, width), lambda i: (0, 0)),
        ],
        out_specs=[
            pl.BlockSpec((UP_SENDERS, rows, width), lambda i: (i, 0, 0)),
            pl.BlockSpec((UP_SENDERS, 1, rows), lambda i: (i, 0, 0)),
        ],
        out_shape=[
            pltpu.HBM((dp_count, rows, width), bf16),
            jax.ShapeDtypeStruct((dp_count, 1, rows), f32),
        ],
        compiler_params=pltpu.CompilerParams(vmem_limit_bytes=VMEM_GRANT),
        cost_estimate=pl.CostEstimate(
            flops=4 * rows * width * hidden * dp_count,
            bytes_accessed=2 * rows * width * dp_count,
            transcendentals=0,
        ),
    )(packed, scale_a, scale_b, scale_g, gate_weight[0].T, up_weight[0].T)
    routed = lax.psum_scatter(
        part.reshape(dp_count * rows, width), "dp", scatter_dimension=0, tiled=True
    )

    records = packed[:, hidden + hidden // 2 :, :expert_count].astype(f32)
    member = records[:, 0] == pieces[0]
    scores = jnp.where(member, records[:, 1] + records[:, 2] + records[:, 3], NEG)
    risks = (records[:, 4] * 128.0 + records[:, 5]) * 0.001
    peak = jnp.max(scores)
    lifted = jnp.where(member, jnp.exp(scores - peak), 0.0)
    mass = jnp.sum(lifted)
    loaded = jnp.sum(lifted * risks)
    risk_value = points.astype(f32) * 0.001
    cand_weight = jnp.exp(score - peak) / mass * (risk_value - loaded / mass)

    gate_sum = lax.all_to_all(gate_parts, "dp", split_axis=0, concat_axis=0, tiled=True)
    gate_sum = jnp.sum(gate_sum, axis=0).reshape(expert_count, 1, cap)
    home_grad = lax.all_to_all(gate_sum, "expert", split_axis=0, concat_axis=0, tiled=True)
    home_grad = home_grad.reshape(rows).astype(bf16)
    placer = (
        jnp.arange(rows, dtype=jnp.int32)[:, None] == (chosen * cap + slot_rank)[None, :]
    ).astype(bf16)
    grad_tok = jnp.einsum("st,s->t", placer, home_grad, preferred_element_type=f32)

    chosen_mark = one_hot.astype(f32)
    peak_logit = jnp.max(router_logits, axis=1, keepdims=True)
    expd = jnp.exp(router_logits - peak_logit)
    router_prob = expd / jnp.sum(expd, axis=1, keepdims=True)
    chosen_prob = jnp.sum(router_prob * chosen_mark, axis=1) * cand_weight
    logit_grad = ((grad_tok * chosen_prob)[:, None] * (chosen_mark - router_prob)).astype(bf16)

    router_part = jnp.einsum("td,te->de", layer_input, logit_grad, preferred_element_type=f32)
    share = width // expert_count
    router_part = router_part.reshape(expert_count, share, experts)
    router_part = lax.all_to_all(router_part, "expert", split_axis=0, concat_axis=0, tiled=True)
    router_part = jnp.sum(router_part, axis=0).reshape(dp_count, share // dp_count, experts)
    router_part = lax.all_to_all(router_part, "dp", split_axis=0, concat_axis=0, tiled=True)
    router_grad = jnp.sum(router_part, axis=0).T

    router_term = jnp.dot(logit_grad, router_weight, preferred_element_type=f32)
    routed, router_grad, router_term, chosen_prob, placer = lax.optimization_barrier(
        (routed, router_grad, router_term, chosen_prob, placer)
    )
    homeward = lax.all_to_all(
        routed.reshape(expert_count, rows * width // expert_count // LANES, LANES),
        "expert",
        split_axis=0,
        concat_axis=0,
        tiled=True,
    )
    routed_tok = jnp.einsum(
        "st,sd->td", placer, homeward.reshape(rows, width), preferred_element_type=f32
    )
    input_grad = (chosen_prob[:, None] * routed_tok + router_term).astype(bf16)
    return (input_grad, router_grad)


def solution(mesh):
    return jax.shard_map(
        local,
        mesh=mesh,
        in_specs=(
            P(("expert", "dp"), None),
            P(("expert", "dp"), None),
            P(("expert", "dp"), None),
            P(("expert", "dp"), None),
            P(),
            P("expert", None, "dp"),
            P("expert", None, "dp"),
            P("expert", "dp", None),
            P("expert", None, None, None, None, "dp"),
            P(("expert", "dp")),
            P(("expert", "dp")),
            P(("expert", "dp")),
        ),
        out_specs=(P(("expert", "dp"), None), P(None, ("expert", "dp"))),
        check_vma=False,
    )
```

```python
import functools

import jax
import jax.numpy as jnp
from jax import lax
from jax.experimental import pallas as pl
from jax.experimental.pallas import tpu as pltpu
from jax.sharding import PartitionSpec as P

NEG = -1e30
LANES = 128
RECORD_ROWS = 8
DOWN_PIECES = 4
DOWN_HOLDERS = 4
UP_CHUNKS = 2
VMEM_GRANT = 32 * 2**20


def nt_dot(left, right):
    return lax.dot_general(left, right, (((1,), (1,)), ((), ())), preferred_element_type=jnp.float32)


def down_kernel(*refs):
    *down_refs, rows_ref, record_ref, out_ref = refs
    holders = out_ref.shape[0]
    hidden = down_refs[0].shape[0] // holders
    half = hidden // 2
    span = down_refs[0].shape[1]
    bf16 = jnp.bfloat16
    full = sum(
        nt_dot(ref[...], rows_ref[:, place * span : (place + 1) * span])
        for place, ref in enumerate(down_refs)
    )
    pick = (
        lax.broadcasted_iota(jnp.int32, (RECORD_ROWS, LANES), 0)
        == lax.broadcasted_iota(jnp.int32, (RECORD_ROWS, LANES), 1)
    ).astype(bf16)
    record = nt_dot(pick, record_ref[...])
    record = jnp.concatenate([record, jnp.zeros_like(record)], axis=1)
    for holder in range(holders):
        block = full[holder * hidden : (holder + 1) * hidden]
        tail = block[:, LANES:]
        tail = jnp.concatenate([tail[:half], tail[half:]], axis=1)
        out_ref[holder, :hidden, :] = block[:, :LANES].astype(bf16)
        out_ref[holder, hidden:, :] = jnp.concatenate([tail, record], axis=0).astype(bf16)


def up_kernel(
    packed_ref,
    scale_a_ref,
    scale_b_ref,
    scale_g_ref,
    gate_ref,
    up_ref,
    part_ref,
    gate_part_ref,
    held,
    sems,
):
    senders = packed_ref.shape[0]
    hidden, width = gate_ref.shape
    half = hidden // 2
    seam = LANES // 2
    span = width // UP_CHUNKS
    f32, bf16 = jnp.float32, jnp.bfloat16
    copies = []
    for sender in range(senders):
        head = packed_ref[sender, :hidden, :].astype(f32)
        tail = packed_ref[sender, hidden:, :].astype(f32)[:half]
        tail = jnp.concatenate([tail[:, :seam], tail[:, seam:]], axis=0)
        down_grad = jnp.concatenate([head, tail], axis=1)
        gate_part_ref[sender] = jnp.sum(down_grad * scale_g_ref[sender], axis=0, keepdims=True)
        grad_a = jnp.transpose(down_grad * scale_a_ref[sender]).astype(bf16)
        grad_b = jnp.transpose(down_grad * scale_b_ref[sender]).astype(bf16)
        for chunk in range(UP_CHUNKS):
            columns = slice(chunk * span, (chunk + 1) * span)
            part = jnp.dot(grad_a, gate_ref[:, columns], preferred_element_type=f32)
            part = part + jnp.dot(grad_b, up_ref[:, columns], preferred_element_type=f32)
            held[sender, :, columns] = part.astype(bf16)
            copy = pltpu.make_async_copy(
                held.at[sender, :, pl.ds(chunk * span, span)],
                part_ref.at[sender, :, pl.ds(chunk * span, span)],
                sems.at[sender, chunk],
            )
            copy.start()
            copies.append(copy)
    for copy in copies:
        copy.wait()


def piece_index(place, i):
    return (i, place)


def local(
    layer_input,
    log_grad,
    router_logits,
    expert_ids,
    router_weight,
    gate_weight,
    up_weight,
    down_weight,
    saved_pre,
    request_ids,
    risk_points,
    cand_scores,
):
    expert_count = lax.axis_size("expert")
    dp_count = lax.axis_size("dp")
    experts = router_weight.shape[0]
    cap = saved_pre.shape[3]
    hidden = saved_pre.shape[5]
    width = layer_input.shape[1]
    rows = expert_count * cap
    packed_rows = hidden + hidden // 2 + RECORD_ROWS
    f32, bf16 = jnp.float32, jnp.bfloat16

    down_full = lax.all_gather(down_weight[0], "dp", axis=0, tiled=True)

    score = cand_scores[0]
    score_hi = lax.reduce_precision(score, 8, 7)
    score_mid = lax.reduce_precision(score - score_hi, 8, 7)
    score_lo = lax.reduce_precision(score - score_hi - score_mid, 8, 7)
    points = risk_points[0]
    pieces = (
        request_ids[0].astype(f32),
        score_hi,
        score_mid,
        score_lo,
        (points // 128).astype(f32),
        (points % 128).astype(f32),
    )
    lane = jnp.arange(width, dtype=jnp.int32)
    record = jnp.zeros((width,), f32)
    for place, piece in enumerate(pieces):
        record = jnp.where(lane == place, piece, record)

    chosen = expert_ids[:, 0]
    one_hot = (chosen[:, None] == jnp.arange(experts, dtype=jnp.int32)[None, :]).astype(jnp.int32)
    slot_rank = jnp.sum(one_hot * (jnp.cumsum(one_hot, axis=0) - 1), axis=1)
    line = jnp.arange(experts * (cap + 1), dtype=jnp.int32)
    spread = (line[:, None] == (chosen * (cap + 1) + slot_rank)[None, :]).astype(bf16)
    outgoing = jnp.dot(spread, log_grad, preferred_element_type=f32)
    outgoing = jnp.where((line % (cap + 1) == cap)[:, None], record[None, :], outgoing)
    outgoing = outgoing.astype(bf16).reshape(experts, cap + 1, width)
    arrived = lax.all_to_all(outgoing, "expert", split_axis=0, concat_axis=0, tiled=True)
    slot_rows = arrived[:, :cap].reshape(rows, width)
    record_rows = arrived[:, cap, :LANES]

    saved = jnp.transpose(saved_pre[0], (3, 1, 4, 0, 2)).reshape(2, dp_count, hidden, rows)
    gate_pre = saved[0].astype(f32)
    up_pre = saved[1].astype(f32)
    sigmoid_a = jax.nn.sigmoid(gate_pre)
    scale_b = gate_pre * sigmoid_a
    scale_g = scale_b * up_pre
    scale_a = up_pre * sigmoid_a * (1.0 + gate_pre * (1.0 - sigmoid_a))
    slot_rows, record_rows, scale_a, scale_b, scale_g, down_full = lax.optimization_barrier(
        (slot_rows, record_rows, scale_a, scale_b, scale_g, down_full)
    )

    span = width // DOWN_PIECES
    packed = pl.pallas_call(
        down_kernel,
        grid=(dp_count // DOWN_HOLDERS,),
        in_specs=[
            pl.BlockSpec((DOWN_HOLDERS * hidden, span), functools.partial(piece_index, place))
            for place in range(DOWN_PIECES)
        ]
        + [
            pl.BlockSpec((rows, width), lambda i: (0, 0)),
            pl.BlockSpec((expert_count, LANES), lambda i: (0, 0)),
        ],
        out_specs=pl.BlockSpec((DOWN_HOLDERS, packed_rows, LANES), lambda i: (i, 0, 0)),
        out_shape=jax.ShapeDtypeStruct((dp_count, packed_rows, LANES), bf16),
        compiler_params=pltpu.CompilerParams(vmem_limit_bytes=VMEM_GRANT),
        cost_estimate=pl.CostEstimate(
            flops=2 * rows * width * hidden * dp_count,
            bytes_accessed=2 * width * hidden * dp_count,
            transcendentals=0,
        ),
    )(
        *[pltpu.with_memory_space_constraint(down_full, pltpu.HBM)] * DOWN_PIECES,
        slot_rows,
        record_rows,
    )
    packed = lax.all_to_all(packed, "dp", split_axis=0, concat_axis=0, tiled=True)

    part, gate_parts = pl.pallas_call(
        up_kernel,
        in_specs=[pl.BlockSpec(memory_space=pltpu.VMEM)] * 6,
        out_specs=[
            pl.BlockSpec(memory_space=pl.ANY),
            pl.BlockSpec(memory_space=pltpu.VMEM),
        ],
        scratch_shapes=[
            pltpu.VMEM((dp_count, rows, width), bf16),
            pltpu.SemaphoreType.DMA((dp_count, UP_CHUNKS)),
        ],
        out_shape=[
            pltpu.HBM((dp_count, rows, width), bf16),
            jax.ShapeDtypeStruct((dp_count, 1, rows), f32),
        ],
        compiler_params=pltpu.CompilerParams(vmem_limit_bytes=VMEM_GRANT),
        cost_estimate=pl.CostEstimate(
            flops=4 * rows * width * hidden * dp_count,
            bytes_accessed=2 * rows * width * dp_count,
            transcendentals=0,
        ),
    )(packed, scale_a, scale_b, scale_g, gate_weight[0].T, up_weight[0].T)
    routed = lax.psum_scatter(
        part.reshape(dp_count * rows, width), "dp", scatter_dimension=0, tiled=True
    )

    records = packed[:, hidden + hidden // 2 :, :expert_count].astype(f32)
    member = records[:, 0] == pieces[0]
    scores = jnp.where(member, records[:, 1] + records[:, 2] + records[:, 3], NEG)
    risks = (records[:, 4] * 128.0 + records[:, 5]) * 0.001
    peak = jnp.max(scores)
    lifted = jnp.where(member, jnp.exp(scores - peak), 0.0)
    mass = jnp.sum(lifted)
    loaded = jnp.sum(lifted * risks)
    risk_value = points.astype(f32) * 0.001
    cand_weight = jnp.exp(score - peak) / mass * (risk_value - loaded / mass)

    gate_sum = lax.all_to_all(gate_parts, "dp", split_axis=0, concat_axis=0, tiled=True)
    gate_sum = jnp.sum(gate_sum, axis=0).reshape(expert_count, 1, cap)
    home_grad = lax.all_to_all(gate_sum, "expert", split_axis=0, concat_axis=0, tiled=True)
    home_grad = home_grad.reshape(rows).astype(bf16)
    placer = (
        jnp.arange(rows, dtype=jnp.int32)[:, None] == (chosen * cap + slot_rank)[None, :]
    ).astype(bf16)
    grad_tok = jnp.einsum("st,s->t", placer, home_grad, preferred_element_type=f32)

    chosen_mark = one_hot.astype(f32)
    peak_logit = jnp.max(router_logits, axis=1, keepdims=True)
    expd = jnp.exp(router_logits - peak_logit)
    router_prob = expd / jnp.sum(expd, axis=1, keepdims=True)
    chosen_prob = jnp.sum(router_prob * chosen_mark, axis=1) * cand_weight
    logit_grad = ((grad_tok * chosen_prob)[:, None] * (chosen_mark - router_prob)).astype(bf16)

    router_part = jnp.einsum("td,te->de", layer_input, logit_grad, preferred_element_type=f32)
    share = width // expert_count
    router_part = router_part.reshape(expert_count, share, experts)
    router_part = lax.all_to_all(router_part, "expert", split_axis=0, concat_axis=0, tiled=True)
    router_part = jnp.sum(router_part, axis=0).reshape(dp_count, share // dp_count, experts)
    router_part = lax.all_to_all(router_part, "dp", split_axis=0, concat_axis=0, tiled=True)
    router_grad = jnp.sum(router_part, axis=0).T

    router_term = jnp.dot(logit_grad, router_weight, preferred_element_type=f32)
    routed, router_grad, router_term, chosen_prob, placer = lax.optimization_barrier(
        (routed, router_grad, router_term, chosen_prob, placer)
    )
    homeward = lax.all_to_all(
        routed.reshape(expert_count, rows * width // expert_count // LANES, LANES),
        "expert",
        split_axis=0,
        concat_axis=0,
        tiled=True,
    )
    routed_tok = jnp.einsum(
        "st,sd->td", placer, homeward.reshape(rows, width), preferred_element_type=f32
    )
    input_grad = (chosen_prob[:, None] * routed_tok + router_term).astype(bf16)
    return (input_grad, router_grad)


def solution(mesh):
    return jax.shard_map(
        local,
        mesh=mesh,
        in_specs=(
            P(("expert", "dp"), None),
            P(("expert", "dp"), None),
            P(("expert", "dp"), None),
            P(("expert", "dp"), None),
            P(),
            P("expert", None, "dp"),
            P("expert", None, "dp"),
            P("expert", "dp", None),
            P("expert", None, None, None, None, "dp"),
            P(("expert", "dp")),
            P(("expert", "dp")),
            P(("expert", "dp")),
        ),
        out_specs=(P(("expert", "dp"), None), P(None, ("expert", "dp"))),
        check_vma=False,
    )
```

```python
import functools

import jax
import jax.numpy as jnp
from jax import lax
from jax.experimental import pallas as pl
from jax.experimental.pallas import tpu as pltpu
from jax.sharding import PartitionSpec as P

NEG = -1e30
LANES = 128
RECORD_ROWS = 8
DOWN_PIECES = 4
DOWN_HOLDERS = 4
UP_CHUNKS = 2
VMEM_GRANT = 32 * 2**20


def nt_dot(left, right):
    return lax.dot_general(left, right, (((1,), (1,)), ((), ())), preferred_element_type=jnp.float32)


def down_kernel(*refs):
    *down_refs, rows_ref, record_ref, out_ref = refs
    holders = out_ref.shape[0]
    hidden = down_refs[0].shape[0] // holders
    half = hidden // 2
    span = down_refs[0].shape[1]
    bf16 = jnp.bfloat16
    full = sum(
        nt_dot(ref[...], rows_ref[:, place * span : (place + 1) * span])
        for place, ref in enumerate(down_refs)
    )
    pick = (
        lax.broadcasted_iota(jnp.int32, (RECORD_ROWS, LANES), 0)
        == lax.broadcasted_iota(jnp.int32, (RECORD_ROWS, LANES), 1)
    ).astype(bf16)
    record = nt_dot(pick, record_ref[...])
    record = jnp.concatenate([record, jnp.zeros_like(record)], axis=1)
    for holder in range(holders):
        block = full[holder * hidden : (holder + 1) * hidden]
        tail = block[:, LANES:]
        tail = jnp.concatenate([tail[:half], tail[half:]], axis=1)
        out_ref[holder, :hidden, :] = block[:, :LANES].astype(bf16)
        out_ref[holder, hidden:, :] = jnp.concatenate([tail, record], axis=0).astype(bf16)


def up_kernel(
    packed_ref,
    scale_a_ref,
    scale_b_ref,
    scale_g_ref,
    gate_ref,
    up_ref,
    part_ref,
    gate_part_ref,
    held,
    sems,
):
    senders = packed_ref.shape[0]
    hidden, width = gate_ref.shape
    half = hidden // 2
    seam = LANES // 2
    span = width // UP_CHUNKS
    f32, bf16 = jnp.float32, jnp.bfloat16
    copies = []
    for sender in range(senders):
        head = packed_ref[sender, :hidden, :].astype(f32)
        tail = packed_ref[sender, hidden:, :].astype(f32)[:half]
        tail = jnp.concatenate([tail[:, :seam], tail[:, seam:]], axis=0)
        down_grad = jnp.concatenate([head, tail], axis=1)
        gate_part_ref[sender] = jnp.sum(down_grad * scale_g_ref[sender], axis=0, keepdims=True)
        grad_a = jnp.transpose(down_grad * scale_a_ref[sender]).astype(bf16)
        grad_b = jnp.transpose(down_grad * scale_b_ref[sender]).astype(bf16)
        for chunk in range(UP_CHUNKS):
            columns = slice(chunk * span, (chunk + 1) * span)
            part = jnp.dot(grad_a, gate_ref[:, columns], preferred_element_type=f32)
            part = part + jnp.dot(grad_b, up_ref[:, columns], preferred_element_type=f32)
            held[sender, :, columns] = part.astype(bf16)
            copy = pltpu.make_async_copy(
                held.at[sender, :, pl.ds(chunk * span, span)],
                part_ref.at[sender, :, pl.ds(chunk * span, span)],
                sems.at[sender, chunk],
            )
            copy.start()
            copies.append(copy)
    for copy in copies:
        copy.wait()


def piece_index(place, i):
    return (i, place)


def local(
    layer_input,
    log_grad,
    router_logits,
    expert_ids,
    router_weight,
    gate_weight,
    up_weight,
    down_weight,
    saved_pre,
    request_ids,
    risk_points,
    cand_scores,
):
    expert_count = lax.axis_size("expert")
    dp_count = lax.axis_size("dp")
    experts = router_weight.shape[0]
    cap = saved_pre.shape[3]
    hidden = saved_pre.shape[5]
    width = layer_input.shape[1]
    rows = expert_count * cap
    packed_rows = hidden + hidden // 2 + RECORD_ROWS
    f32, bf16 = jnp.float32, jnp.bfloat16

    down_full = lax.all_gather(down_weight[0], "dp", axis=0, tiled=True)

    score = cand_scores[0]
    score_hi = lax.reduce_precision(score, 8, 7)
    score_mid = lax.reduce_precision(score - score_hi, 8, 7)
    score_lo = lax.reduce_precision(score - score_hi - score_mid, 8, 7)
    points = risk_points[0]
    pieces = (
        request_ids[0].astype(f32),
        score_hi,
        score_mid,
        score_lo,
        (points // 128).astype(f32),
        (points % 128).astype(f32),
    )
    lane = jnp.arange(width, dtype=jnp.int32)
    record = jnp.zeros((width,), f32)
    for place, piece in enumerate(pieces):
        record = jnp.where(lane == place, piece, record)

    chosen = expert_ids[:, 0]
    one_hot = (chosen[:, None] == jnp.arange(experts, dtype=jnp.int32)[None, :]).astype(jnp.int32)
    slot_rank = jnp.sum(one_hot * (jnp.cumsum(one_hot, axis=0) - 1), axis=1)
    line = jnp.arange(experts * (cap + 1), dtype=jnp.int32)
    spread = (line[:, None] == (chosen * (cap + 1) + slot_rank)[None, :]).astype(bf16)
    outgoing = jnp.dot(spread, log_grad, preferred_element_type=f32)
    outgoing = jnp.where((line % (cap + 1) == cap)[:, None], record[None, :], outgoing)
    outgoing = outgoing.astype(bf16).reshape(experts, cap + 1, width)
    arrived = lax.all_to_all(outgoing, "expert", split_axis=0, concat_axis=0, tiled=True)
    slot_rows = arrived[:, :cap].reshape(rows, width)
    record_rows = arrived[:, cap, :LANES]

    saved = jnp.transpose(saved_pre[0], (3, 1, 4, 0, 2)).reshape(2, dp_count, hidden, rows)
    gate_pre = saved[0].astype(f32)
    up_pre = saved[1].astype(f32)
    sigmoid_a = jax.nn.sigmoid(gate_pre)
    scale_b = gate_pre * sigmoid_a
    scale_g = scale_b * up_pre
    scale_a = up_pre * sigmoid_a * (1.0 + gate_pre * (1.0 - sigmoid_a))
    slot_rows, record_rows, scale_a, scale_b, scale_g, down_full = lax.optimization_barrier(
        (slot_rows, record_rows, scale_a, scale_b, scale_g, down_full)
    )

    span = width // DOWN_PIECES
    packed = pl.pallas_call(
        down_kernel,
        grid=(dp_count // DOWN_HOLDERS,),
        in_specs=[
            pl.BlockSpec((DOWN_HOLDERS * hidden, span), functools.partial(piece_index, place))
            for place in range(DOWN_PIECES)
        ]
        + [
            pl.BlockSpec((rows, width), lambda i: (0, 0)),
            pl.BlockSpec((expert_count, LANES), lambda i: (0, 0)),
        ],
        out_specs=pl.BlockSpec((DOWN_HOLDERS, packed_rows, LANES), lambda i: (i, 0, 0)),
        out_shape=jax.ShapeDtypeStruct((dp_count, packed_rows, LANES), bf16),
        compiler_params=pltpu.CompilerParams(vmem_limit_bytes=VMEM_GRANT),
        cost_estimate=pl.CostEstimate(
            flops=2 * rows * width * hidden * dp_count,
            bytes_accessed=2 * width * hidden * dp_count,
            transcendentals=0,
        ),
    )(
        *[pltpu.with_memory_space_constraint(down_full, pltpu.HBM)] * DOWN_PIECES,
        slot_rows,
        record_rows,
    )
    packed = lax.all_to_all(packed, "dp", split_axis=0, concat_axis=0, tiled=True)

    part, gate_parts = pl.pallas_call(
        up_kernel,
        in_specs=[pl.BlockSpec(memory_space=pltpu.VMEM)] * 6,
        out_specs=[
            pl.BlockSpec(memory_space=pl.ANY),
            pl.BlockSpec(memory_space=pltpu.VMEM),
        ],
        scratch_shapes=[
            pltpu.VMEM((dp_count, rows, width), bf16),
            pltpu.SemaphoreType.DMA((dp_count, UP_CHUNKS)),
        ],
        out_shape=[
            pltpu.HBM((dp_count, rows, width), bf16),
            jax.ShapeDtypeStruct((dp_count, 1, rows), f32),
        ],
        compiler_params=pltpu.CompilerParams(vmem_limit_bytes=VMEM_GRANT),
        cost_estimate=pl.CostEstimate(
            flops=4 * rows * width * hidden * dp_count,
            bytes_accessed=2 * rows * width * dp_count,
            transcendentals=0,
        ),
    )(packed, scale_a, scale_b, scale_g, gate_weight[0].T, up_weight[0].T)
    routed = lax.psum_scatter(
        part.reshape(dp_count * rows, width), "dp", scatter_dimension=0, tiled=True
    )

    records = packed[:, hidden + hidden // 2 :, :expert_count].astype(f32)
    member = records[:, 0] == pieces[0]
    scores = jnp.where(member, records[:, 1] + records[:, 2] + records[:, 3], NEG)
    risks = (records[:, 4] * 128.0 + records[:, 5]) * 0.001
    peak = jnp.max(scores)
    lifted = jnp.where(member, jnp.exp(scores - peak), 0.0)
    mass = jnp.sum(lifted)
    loaded = jnp.sum(lifted * risks)
    risk_value = points.astype(f32) * 0.001
    cand_weight = jnp.exp(score - peak) / mass * (risk_value - loaded / mass)

    gate_sum = lax.all_to_all(gate_parts, "dp", split_axis=0, concat_axis=0, tiled=True)
    gate_sum = jnp.sum(gate_sum, axis=0).reshape(expert_count, 1, cap)
    home_grad = lax.all_to_all(gate_sum, "expert", split_axis=0, concat_axis=0, tiled=True)
    home_grad = home_grad.reshape(rows).astype(bf16)
    placer = (
        jnp.arange(rows, dtype=jnp.int32)[:, None] == (chosen * cap + slot_rank)[None, :]
    ).astype(bf16)
    grad_tok = jnp.einsum("st,s->t", placer, home_grad, preferred_element_type=f32)

    chosen_mark = one_hot.astype(f32)
    peak_logit = jnp.max(router_logits, axis=1, keepdims=True)
    expd = jnp.exp(router_logits - peak_logit)
    router_prob = expd / jnp.sum(expd, axis=1, keepdims=True)
    chosen_prob = jnp.sum(router_prob * chosen_mark, axis=1) * cand_weight
    logit_grad = ((grad_tok * chosen_prob)[:, None] * (chosen_mark - router_prob)).astype(bf16)

    router_part = jnp.einsum("td,te->de", layer_input, logit_grad, preferred_element_type=f32)
    share = width // expert_count
    router_part = router_part.reshape(expert_count, 2, share // 2, experts)
    router_part = jnp.concatenate([router_part[:, 0], router_part[:, 1]], axis=2)
    router_part = lax.all_to_all(router_part, "expert", split_axis=0, concat_axis=0, tiled=True)
    router_part = jnp.sum(router_part, axis=0)
    router_part = jnp.concatenate(
        [router_part[:, :experts], router_part[:, experts:]], axis=0
    ).reshape(dp_count, share // dp_count, experts)
    router_part = lax.all_to_all(router_part, "dp", split_axis=0, concat_axis=0, tiled=True)
    router_grad = jnp.sum(router_part, axis=0).T

    router_term = jnp.dot(logit_grad, router_weight, preferred_element_type=f32)
    routed, router_grad, router_term, chosen_prob, placer = lax.optimization_barrier(
        (routed, router_grad, router_term, chosen_prob, placer)
    )
    homeward = lax.all_to_all(
        routed.reshape(expert_count, rows * width // expert_count // LANES, LANES),
        "expert",
        split_axis=0,
        concat_axis=0,
        tiled=True,
    )
    routed_tok = jnp.einsum(
        "st,sd->td", placer, homeward.reshape(rows, width), preferred_element_type=f32
    )
    input_grad = (chosen_prob[:, None] * routed_tok + router_term).astype(bf16)
    return (input_grad, router_grad)


def solution(mesh):
    return jax.shard_map(
        local,
        mesh=mesh,
        in_specs=(
            P(("expert", "dp"), None),
            P(("expert", "dp"), None),
            P(("expert", "dp"), None),
            P(("expert", "dp"), None),
            P(),
            P("expert", None, "dp"),
            P("expert", None, "dp"),
            P("expert", "dp", None),
            P("expert", None, None, None, None, "dp"),
            P(("expert", "dp")),
            P(("expert", "dp")),
            P(("expert", "dp")),
        ),
        out_specs=(P(("expert", "dp"), None), P(None, ("expert", "dp"))),
        check_vma=False,
    )
```

```python
import functools

import jax
import jax.numpy as jnp
from jax import lax
from jax.experimental import pallas as pl
from jax.experimental.pallas import tpu as pltpu
from jax.sharding import PartitionSpec as P

NEG = -1e30
LANES = 128
RECORD_ROWS = 8
DOWN_PIECES = 4
DOWN_HOLDERS = 4
UP_CHUNKS = 1
VMEM_GRANT = 32 * 2**20


def nt_dot(left, right):
    return lax.dot_general(left, right, (((1,), (1,)), ((), ())), preferred_element_type=jnp.float32)


def down_kernel(*refs):
    *down_refs, rows_ref, record_ref, out_ref = refs
    holders = out_ref.shape[0]
    hidden = down_refs[0].shape[0] // holders
    half = hidden // 2
    span = down_refs[0].shape[1]
    bf16 = jnp.bfloat16
    full = sum(
        nt_dot(ref[...], rows_ref[:, place * span : (place + 1) * span])
        for place, ref in enumerate(down_refs)
    )
    pick = (
        lax.broadcasted_iota(jnp.int32, (RECORD_ROWS, LANES), 0)
        == lax.broadcasted_iota(jnp.int32, (RECORD_ROWS, LANES), 1)
    ).astype(bf16)
    record = nt_dot(pick, record_ref[...])
    record = jnp.concatenate([record, jnp.zeros_like(record)], axis=1)
    for holder in range(holders):
        block = full[holder * hidden : (holder + 1) * hidden]
        tail = block[:, LANES:]
        tail = jnp.concatenate([tail[:half], tail[half:]], axis=1)
        out_ref[holder, :hidden, :] = block[:, :LANES].astype(bf16)
        out_ref[holder, hidden:, :] = jnp.concatenate([tail, record], axis=0).astype(bf16)


def up_kernel(
    packed_ref,
    scale_a_ref,
    scale_b_ref,
    scale_g_ref,
    gate_ref,
    up_ref,
    part_ref,
    gate_part_ref,
    held,
    sems,
):
    senders = packed_ref.shape[0]
    hidden, width = gate_ref.shape
    half = hidden // 2
    seam = LANES // 2
    span = width // UP_CHUNKS
    f32, bf16 = jnp.float32, jnp.bfloat16
    copies = []
    for sender in range(senders):
        head = packed_ref[sender, :hidden, :].astype(f32)
        tail = packed_ref[sender, hidden:, :].astype(f32)[:half]
        tail = jnp.concatenate([tail[:, :seam], tail[:, seam:]], axis=0)
        down_grad = jnp.concatenate([head, tail], axis=1)
        gate_part_ref[sender] = jnp.sum(down_grad * scale_g_ref[sender], axis=0, keepdims=True)
        grad_a = jnp.transpose((down_grad * scale_a_ref[sender]).astype(bf16))
        grad_b = jnp.transpose((down_grad * scale_b_ref[sender]).astype(bf16))
        for chunk in range(UP_CHUNKS):
            columns = slice(chunk * span, (chunk + 1) * span)
            part = jnp.dot(grad_a, gate_ref[:, columns], preferred_element_type=f32)
            part = part + jnp.dot(grad_b, up_ref[:, columns], preferred_element_type=f32)
            held[sender, :, columns] = part.astype(bf16)
            copy = pltpu.make_async_copy(
                held.at[sender, :, pl.ds(chunk * span, span)],
                part_ref.at[sender, :, pl.ds(chunk * span, span)],
                sems.at[sender, chunk],
            )
            copy.start()
            copies.append(copy)
    for copy in copies:
        copy.wait()


def piece_index(place, i):
    return (i, place)


def local(
    layer_input,
    log_grad,
    router_logits,
    expert_ids,
    router_weight,
    gate_weight,
    up_weight,
    down_weight,
    saved_pre,
    request_ids,
    risk_points,
    cand_scores,
):
    expert_count = lax.axis_size("expert")
    dp_count = lax.axis_size("dp")
    experts = router_weight.shape[0]
    cap = saved_pre.shape[3]
    hidden = saved_pre.shape[5]
    width = layer_input.shape[1]
    rows = expert_count * cap
    packed_rows = hidden + hidden // 2 + RECORD_ROWS
    f32, bf16 = jnp.float32, jnp.bfloat16

    down_full = lax.all_gather(down_weight[0], "dp", axis=0, tiled=True)

    score = cand_scores[0]
    score_hi = lax.reduce_precision(score, 8, 7)
    score_mid = lax.reduce_precision(score - score_hi, 8, 7)
    score_lo = lax.reduce_precision(score - score_hi - score_mid, 8, 7)
    points = risk_points[0]
    pieces = (
        request_ids[0].astype(f32),
        score_hi,
        score_mid,
        score_lo,
        (points // 128).astype(f32),
        (points % 128).astype(f32),
    )
    lane = jnp.arange(width, dtype=jnp.int32)
    record = jnp.zeros((width,), f32)
    for place, piece in enumerate(pieces):
        record = jnp.where(lane == place, piece, record)

    chosen = expert_ids[:, 0]
    one_hot = (chosen[:, None] == jnp.arange(experts, dtype=jnp.int32)[None, :]).astype(jnp.int32)
    slot_rank = jnp.sum(one_hot * (jnp.cumsum(one_hot, axis=0) - 1), axis=1)
    line = jnp.arange(experts * (cap + 1), dtype=jnp.int32)
    spread = (line[:, None] == (chosen * (cap + 1) + slot_rank)[None, :]).astype(bf16)
    outgoing = jnp.dot(spread, log_grad, preferred_element_type=f32)
    outgoing = jnp.where((line % (cap + 1) == cap)[:, None], record[None, :], outgoing)
    outgoing = outgoing.astype(bf16).reshape(experts, cap + 1, width)
    arrived = lax.all_to_all(outgoing, "expert", split_axis=0, concat_axis=0, tiled=True)
    slot_rows = arrived[:, :cap].reshape(rows, width)
    record_rows = arrived[:, cap, :LANES]

    saved = jnp.transpose(saved_pre[0], (3, 1, 4, 0, 2)).reshape(2, dp_count, hidden, rows)
    gate_pre = saved[0].astype(f32)
    up_pre = saved[1].astype(f32)
    sigmoid_a = jax.nn.sigmoid(gate_pre)
    scale_b = gate_pre * sigmoid_a
    scale_g = scale_b * up_pre
    scale_a = up_pre * sigmoid_a * (1.0 + gate_pre * (1.0 - sigmoid_a))
    slot_rows, record_rows, scale_a, scale_b, scale_g, down_full = lax.optimization_barrier(
        (slot_rows, record_rows, scale_a, scale_b, scale_g, down_full)
    )

    span = width // DOWN_PIECES
    packed = pl.pallas_call(
        down_kernel,
        grid=(dp_count // DOWN_HOLDERS,),
        in_specs=[
            pl.BlockSpec((DOWN_HOLDERS * hidden, span), functools.partial(piece_index, place))
            for place in range(DOWN_PIECES)
        ]
        + [
            pl.BlockSpec((rows, width), lambda i: (0, 0)),
            pl.BlockSpec((expert_count, LANES), lambda i: (0, 0)),
        ],
        out_specs=pl.BlockSpec((DOWN_HOLDERS, packed_rows, LANES), lambda i: (i, 0, 0)),
        out_shape=jax.ShapeDtypeStruct((dp_count, packed_rows, LANES), bf16),
        compiler_params=pltpu.CompilerParams(vmem_limit_bytes=VMEM_GRANT),
        cost_estimate=pl.CostEstimate(
            flops=2 * rows * width * hidden * dp_count,
            bytes_accessed=2 * width * hidden * dp_count,
            transcendentals=0,
        ),
    )(
        *[pltpu.with_memory_space_constraint(down_full, pltpu.HBM)] * DOWN_PIECES,
        slot_rows,
        record_rows,
    )
    packed = lax.all_to_all(packed, "dp", split_axis=0, concat_axis=0, tiled=True)

    part, gate_parts = pl.pallas_call(
        up_kernel,
        in_specs=[pl.BlockSpec(memory_space=pltpu.VMEM)] * 6,
        out_specs=[
            pl.BlockSpec(memory_space=pl.ANY),
            pl.BlockSpec(memory_space=pltpu.VMEM),
        ],
        scratch_shapes=[
            pltpu.VMEM((dp_count, rows, width), bf16),
            pltpu.SemaphoreType.DMA((dp_count, UP_CHUNKS)),
        ],
        out_shape=[
            pltpu.HBM((dp_count, rows, width), bf16),
            jax.ShapeDtypeStruct((dp_count, 1, rows), f32),
        ],
        compiler_params=pltpu.CompilerParams(vmem_limit_bytes=VMEM_GRANT),
        cost_estimate=pl.CostEstimate(
            flops=4 * rows * width * hidden * dp_count,
            bytes_accessed=2 * rows * width * dp_count,
            transcendentals=0,
        ),
    )(packed, scale_a, scale_b, scale_g, gate_weight[0].T, up_weight[0].T)
    routed = lax.psum_scatter(
        part.reshape(dp_count * rows, width), "dp", scatter_dimension=0, tiled=True
    )

    records = packed[:, hidden + hidden // 2 :, :expert_count].astype(f32)
    member = records[:, 0] == pieces[0]
    scores = jnp.where(member, records[:, 1] + records[:, 2] + records[:, 3], NEG)
    risks = (records[:, 4] * 128.0 + records[:, 5]) * 0.001
    peak = jnp.max(scores)
    lifted = jnp.where(member, jnp.exp(scores - peak), 0.0)
    mass = jnp.sum(lifted)
    loaded = jnp.sum(lifted * risks)
    risk_value = points.astype(f32) * 0.001
    cand_weight = jnp.exp(score - peak) / mass * (risk_value - loaded / mass)

    gate_sum = lax.all_to_all(gate_parts, "dp", split_axis=0, concat_axis=0, tiled=True)
    gate_sum = jnp.sum(gate_sum, axis=0).reshape(expert_count, 1, cap)
    home_grad = lax.all_to_all(gate_sum, "expert", split_axis=0, concat_axis=0, tiled=True)
    home_grad = home_grad.reshape(rows).astype(bf16)
    placer = (
        jnp.arange(rows, dtype=jnp.int32)[:, None] == (chosen * cap + slot_rank)[None, :]
    ).astype(bf16)
    grad_tok = jnp.einsum("st,s->t", placer, home_grad, preferred_element_type=f32)

    chosen_mark = one_hot.astype(f32)
    peak_logit = jnp.max(router_logits, axis=1, keepdims=True)
    expd = jnp.exp(router_logits - peak_logit)
    router_prob = expd / jnp.sum(expd, axis=1, keepdims=True)
    chosen_prob = jnp.sum(router_prob * chosen_mark, axis=1) * cand_weight
    logit_grad = ((grad_tok * chosen_prob)[:, None] * (chosen_mark - router_prob)).astype(bf16)

    router_part = jnp.einsum("td,te->de", layer_input, logit_grad, preferred_element_type=f32)
    share = width // expert_count
    router_part = router_part.reshape(expert_count, 2, share // 2, experts)
    router_part = jnp.concatenate([router_part[:, 0], router_part[:, 1]], axis=2)
    router_part = lax.all_to_all(router_part, "expert", split_axis=0, concat_axis=0, tiled=True)
    router_part = jnp.sum(router_part, axis=0)
    router_part = jnp.concatenate(
        [router_part[:, :experts], router_part[:, experts:]], axis=0
    ).reshape(dp_count, share // dp_count, experts)
    router_part = lax.all_to_all(router_part, "dp", split_axis=0, concat_axis=0, tiled=True)
    router_grad = jnp.sum(router_part, axis=0).T

    router_term = jnp.dot(logit_grad, router_weight, preferred_element_type=f32)
    routed, router_grad, router_term, chosen_prob, placer = lax.optimization_barrier(
        (routed, router_grad, router_term, chosen_prob, placer)
    )
    homeward = lax.all_to_all(
        routed.reshape(expert_count, rows * width // expert_count // LANES, LANES),
        "expert",
        split_axis=0,
        concat_axis=0,
        tiled=True,
    )
    routed_tok = jnp.einsum(
        "st,sd->td", placer, homeward.reshape(rows, width), preferred_element_type=f32
    )
    input_grad = (chosen_prob[:, None] * routed_tok + router_term).astype(bf16)
    return (input_grad, router_grad)


def solution(mesh):
    return jax.shard_map(
        local,
        mesh=mesh,
        in_specs=(
            P(("expert", "dp"), None),
            P(("expert", "dp"), None),
            P(("expert", "dp"), None),
            P(("expert", "dp"), None),
            P(),
            P("expert", None, "dp"),
            P("expert", None, "dp"),
            P("expert", "dp", None),
            P("expert", None, None, None, None, "dp"),
            P(("expert", "dp")),
            P(("expert", "dp")),
            P(("expert", "dp")),
        ),
        out_specs=(P(("expert", "dp"), None), P(None, ("expert", "dp"))),
        check_vma=False,
    )
```
